256 devices in a mesh: section: 16 (over z, x_hi), tensor: 16 (over x_lo, y, core).
Axes of the slice: x: 4 (x_hi: 2, x_lo: 2; x = x_hi * 2 + x_lo), y: 4, z: 8, core: 2. Of those that a mesh axis runs over, the one named last changes fastest.
Arguments:
- old_weight: float32 [16, 256, 6144], P('section', 'tensor'), may hold values from -6 to 6
- old_first: float32 [16, 256, 6144], P('section', 'tensor'), may hold values from -6 to 6
- old_second: float32 [16, 256, 6144], P('section', 'tensor'), may hold values from 0.1 to 2
- mixing: float32 [32, 16], replicated, may hold values from -1.5 to 1.5
- target_rms: float32 [32], P('section'), may hold values from 0.5 to 2
Outputs:
- new_weight: float32 [32, 256, 6144], P('section', 'tensor')
- new_first: float32 [32, 256, 6144], P('section', 'tensor')
- new_second: float32 [32, 256, 6144], P('section', 'tensor')
The draws below stay inside these ranges and needn't reach their ends.
All inputs are finite; a program needn't handle non-finite values.
Results may differ from the reference program's by a relative error of at most 0.0003.
Values sent between devices are 32-bit elements; how exact they have to be, the bound alone decides.
A program may use at most 192 MiB of HBM per device.

```python
import math
import jax
import jax.numpy as jnp
from jax import lax

D = 6144
L_OLD = 16
L_NEW = 32
ROWS = 256


def levels(rng, shape, cuts, least, largest):
    level = 1.0
    for position, shards_of in cuts:
        heights = jax.random.uniform(jax.random.fold_in(jax.random.fold_in(rng, 6), position), (shards_of,), jnp.float32, least / len(cuts), largest / len(cuts))
        level = level * jnp.repeat(jnp.exp(heights), shape[position] // shards_of).reshape((-1,) + (1,) * (len(shape) - 1 - position))
    return level


def bell_draw(stream_key, extent, spread, most, pieces=(), held_as=jnp.bfloat16):
    factor_of = levels(stream_key, extent, pieces, -0.22, 0.18) if pieces else 1.0
    entries = jax.random.normal(stream_key, extent, jnp.float32) * spread * factor_of
    return jnp.minimum(jnp.maximum(entries, -most), most).astype(held_as)


def setup_inputs(seed: int = 0) -> dict:
    arg_keys = jax.random.split(jax.random.key(seed), 6)
    return {
        "old_weight": bell_draw(arg_keys[0], (L_OLD, ROWS, D), 1.0, 6.0, ((0, 16), (1, 16)), jnp.float32),
        "old_first": bell_draw(arg_keys[1], (L_OLD, ROWS, D), 1.0, 6.0, ((0, 16), (1, 16)), jnp.float32),
        "old_second": jnp.clip(jnp.exp(math.log(2.0) - 2.9957323 * jax.random.uniform(arg_keys[2], (L_OLD, ROWS, D), jnp.float32) ** levels(arg_keys[2], (L_OLD, ROWS, D), ((0, 16), (1, 16)), -0.2, 0.2)), 0.1, 2.0),
        "mixing": bell_draw(arg_keys[3], (L_NEW, L_OLD), L_OLD ** -0.5, 1.5, (), jnp.float32),
        "target_rms": jnp.clip(jnp.exp(math.log(2.0) - 1.3862944 * jax.random.uniform(arg_keys[4], (L_NEW,), jnp.float32) ** levels(arg_keys[4], (L_NEW,), ((0, 16),), -0.2, 0.2)), 0.5, 2.0),
    }


def combine(coefs, stack):
    flat = stack.reshape(stack.shape[0], -1)
    out = jnp.dot(coefs, flat, precision=lax.Precision.HIGHEST, preferred_element_type=jnp.float32)
    return out.reshape((coefs.shape[0],) + stack.shape[1:])

def reference(old_weight, old_first, old_second, mixing, target_rms):
    mixed_weight = combine(mixing, old_weight)
    mixed_first = combine(mixing, old_first)
    mixed_second = combine(mixing * mixing, old_second)
    power = lax.optimization_barrier(jnp.sum(mixed_weight * mixed_weight, axis=(1, 2)))
    factor = target_rms / jnp.sqrt(power / (ROWS * D) + 1e-06)
    scale = factor[:, None, None]
    return (scale * mixed_weight, scale * mixed_first, scale * scale * mixed_second)
```

```python
import jax
import jax.numpy as jnp
from jax import lax
from jax.experimental import pallas as pl
from jax.experimental.pallas import tpu as pltpu
from jax.sharding import PartitionSpec as P

MESH = pl.DeviceIdType.MESH
F32 = jnp.float32

PLANES = 8
LANES = 128
CHUNK = 1024
ROLES = (5, 4, 3, 2, 1, 0, 7, 6)

SOURCES = {
    0: (("own", 5, 0), ("r1", 3, -1), ("r1", 4, -2), ("l1", 4, 1), ("l2", 3, 2), ("l3", 2, 3), ("l4", 1, 4), ("l4", 0, 5)),
    1: (("own", 4, 0), ("r1", 2, -1), ("r2", 2, -2), ("r2", 3, -3), ("l1", 3, 1), ("l2", 2, 2), ("l3", 1, 3), ("l3", 0, 4)),
    2: (("own", 3, 0), ("r1", 1, -1), ("r2", 1, -2), ("r3", 1, -3), ("r3", 2, -4), ("l1", 2, 1), ("l2", 1, 2), ("l2", 0, 3)),
    3: (("own", 2, 0), ("r1", 0, -1), ("r2", 0, -2), ("r3", 0, -3), ("r4", 0, -4), ("r4", 1, -5), ("l1", 1, 1), ("l1", 0, 2)),
}
TARGETS = {0: ((-2, 0), (-1, 2), (0, 4)), 3: ((2, 1), (1, 3), (0, 5)), 1: ((0, 6),), 2: ((0, 7),)}
FORWARD = {
    2: (("r1", 1, "r2", 4, 1), ("l1", 0, "l2", 4, -1)),
    3: (("r2", 1, "r3", 3, 1), ("l2", 0, "l3", 3, -1)),
    4: (("r3", 1, "r4", 2, 1), ("l3", 0, "l4", 2, -1)),
}
LEAD = 3
LAG = {2: 1, 3: 2, 4: 3, "mix": 4, "join": 5, "end": 6}


def kernel(weight, first, second, mixing, target, mixed, factor, stage, own, r1, r2, r3, r4, l1, l2, l3, l4,
           part, sent, came, back, done, pow_sent, pow_came, in_sem, out_sem, ssem, rsem, pow_ssem, pow_rsem):
    count = own.shape[0]
    per = count // 3
    width = own.shape[3]
    rows = own.shape[2]
    section = lax.axis_index("section")
    tensor = lax.axis_index("tensor")
    z = section // 2
    half = lax.rem(section, 2)
    refs = dict(own=own, r1=r1, r2=r2, r3=r3, r4=r4, l1=l1, l2=l2, l3=l3, l4=l4)

    def plane(step):
        return lax.rem(z + (step + PLANES), PLANES)

    def along(step):
        return (plane(step) * 2 + half, tensor)

    def flip(bit):
        return (section, tensor + bit - 2 * bit * lax.rem(tensor // bit, 2))

    across = (z * 2 + 1 - half, tensor)
    bits = (1, 8, 2, 4)
    partners = [flip(bit) for bit in bits]

    loads = []
    for a, array in enumerate((weight, first, second)):
        for s in range(per):
            c = a * per + s
            loads.append(pltpu.make_async_copy(
                array.at[0, :, pl.ds(s * CHUNK, CHUNK)], stage.at[c], in_sem.at[c]))
    for load in loads:
        load.start()

    barrier = pltpu.get_barrier_semaphore()
    peers = [along(1), along(-1), along(2), along(-2), across] + partners
    for peer in peers:
        pl.semaphore_signal(barrier, inc=1, device_id=peer, device_id_type=MESH)

    for load in loads:
        load.wait()

    def turn(c, _):
        for i in range(PLANES):
            slab = lax.rem(z + (i + 3), PLANES)
            own[c, i] = stage[c, :, pl.ds(pl.multiple_of(slab * width, LANES), width)]
        return 0

    lax.fori_loop(0, count, turn, 0)
    pl.semaphore_wait(barrier, len(peers))

    def remote(src, dst, c, k, device):
        return pltpu.make_async_remote_copy(
            src_ref=src, dst_ref=dst, send_sem=ssem.at[c, k], recv_sem=rsem.at[c, k],
            device_id=device, device_id_type=MESH)

    def step1(c):
        return [
            remote(own.at[c, pl.ds(3, 4)], r1.at[c, pl.ds(0, 4)], c, 0, along(1)),
            remote(own.at[c, pl.ds(7, 1)], r1.at[c, pl.ds(4, 1)], c, 1, along(2)),
            remote(own.at[c, pl.ds(1, 4)], l1.at[c, pl.ds(1, 4)], c, 2, along(-1)),
            remote(own.at[c, pl.ds(0, 1)], l1.at[c, pl.ds(0, 1)], c, 3, along(-2)),
        ]

    def forward(k, c):
        return [
            remote(refs[src].at[c, pl.ds(at, n)], refs[dst].at[c, pl.ds(0, n)], c, 2 * k + i, along(way))
            for i, (src, at, dst, n, way) in enumerate(FORWARD[k])
        ]

    def cross(c):
        return [
            remote(sent.at[c, pl.ds(0, 4)], came.at[c, pl.ds(0, 4)], c, 10, across),
            remote(sent.at[c, pl.ds(4, 2)], came.at[c, pl.ds(4, 2)], c, 11, across),
            remote(sent.at[c, pl.ds(6, 2)], came.at[c, pl.ds(6, 2)], c, 12, across),
        ]

    def give(c):
        return [
            remote(part.at[c, i], back.at[c, i], c, 13 + i, along(way))
            for i, way in enumerate((-2, 2, -1, 1))
        ]

    def mix(c, role):
        squared = c >= 2 * per
        for step, place in TARGETS[role]:
            to = plane(step) * 2
            for lane in range(0, width, LANES):
                lanes = pl.ds(lane, LANES)
                sums = [[None, None], [None, None]]
                for name, at, away in SOURCES[role]:
                    old = refs[name][c, at, :, lanes]
                    layer = plane(away) * 2 + half
                    for other in range(2):
                        to_half = 1 - half if other else half
                        for n in range(2):
                            coef = mixing[2 * (to + to_half) + n, layer]
                            coef = coef * jnp.where(squared, coef, 1.0)
                            term = coef * old
                            sums[other][n] = term if sums[other][n] is None else sums[other][n] + term
                for n in range(2):
                    part[c, place, n, :, lanes] = sums[0][n]
                    sent[c, place, n, :, lanes] = sums[1][n]

    def output(c):
        s = lax.rem(c, per)
        return pltpu.make_async_copy(
            done.at[c], mixed.at[c // per, :, :, pl.ds(pl.multiple_of(s * CHUNK, CHUNK), CHUNK)], out_sem.at[c])

    def finish(c):
        for role in range(PLANES):
            slab = lax.rem(z + (PLANES - role), PLANES)
            lanes = pl.ds(pl.multiple_of(slab * width, LANES), width)
            ref, at = {0: (part, 4), 1: (part, 6), 2: (part, 7), 3: (part, 5),
                       4: (back, 3), 5: (back, 1), 6: (back, 0), 7: (back, 2)}[role]
            done[c, :, :, lanes] = ref[c, at]

    def power(c):
        for n in range(2):
            total = pow_sent[0, n]
            for lane in range(0, CHUNK, LANES):
                for row in range(0, rows, 8):
                    value = done[c, n, pl.ds(row, 8), pl.ds(lane, LANES)]
                    total = total + value * value
            pow_sent[0, n] = total

    def pow_copy(k):
        return pltpu.make_async_remote_copy(
            src_ref=pow_sent.at[k], dst_ref=pow_came.at[k], send_sem=pow_ssem.at[k], recv_sem=pow_rsem.at[k],
            device_id=partners[k], device_id_type=MESH)

    pow_sent[0] = jnp.zeros_like(pow_sent[0])
    for c in range(LEAD):
        for copy in step1(c):
            copy.start()

    pow_turn = LAG["end"] + per - 1

    def turn_of(t, _):
        def at(lag, body):
            c = t - lag

            @pl.when((c >= 0) & (c < count))
            def _():
                body(c)

        def do_end(c):
            for copy in give(c):
                copy.wait()
            finish(c)
            output(c).start()

            @pl.when(c < per)
            def _():
                power(c)

        def do_join(c):
            for copy in cross(c):
                copy.wait()
            for i in range(8):
                part[c, i] = part[c, i] + came[c, i]
            for copy in give(c):
                copy.start()

        def do_mix(c):
            for copy in forward(4, c):
                copy.wait()
            for role in (0, 3):
                mix(c, role)
            copies = cross(c)
            copies[0].start()
            copies[1].start()
            for role in (1, 2):
                mix(c, role)
            copies[2].start()

        def do_forward(k, c):
            before = step1(c) if k == 2 else forward(k - 1, c)
            for copy in before:
                copy.wait()
            for copy in forward(k, c):
                copy.start()

        def do_first(c):
            for copy in step1(c):
                copy.start()

        at(LAG["end"], do_end)
        at(LAG["join"], do_join)
        at(LAG[4], lambda c: do_forward(4, c))
        at(LAG[3], lambda c: do_forward(3, c))
        at(LAG[2], lambda c: do_forward(2, c))
        at(-LEAD, do_first)
        at(LAG["mix"], do_mix)
        for k in range(len(bits) + 1):
            @pl.when(t == pow_turn + k)
            def _(k=k):
                if k > 0:
                    pow_copy(k - 1).wait()
                    pow_sent[k] = pow_sent[k - 1] + pow_came[k - 1]
                if k < len(bits):
                    pow_copy(k).start()
        return 0

    lax.fori_loop(0, count + LAG["end"], turn_of, 0)

    total_count = rows * lax.axis_size("tensor") * CHUNK * per
    for n in range(2):
        total = jnp.sum(pow_sent[len(bits), n], keepdims=True)
        value = target[n] / jnp.sqrt(total / total_count + 1e-06)
        factor[n] = jnp.broadcast_to(value, factor.shape[1:])

    def drain(c, _):
        output(c).wait()
        return 0

    lax.fori_loop(0, count, drain, 0)


def local(old_weight, old_first, old_second, mixing, target_rms):
    rows, columns = old_weight.shape[1:]
    per = columns // CHUNK
    n = 3 * per
    w = CHUNK // PLANES
    hbm = pl.BlockSpec(memory_space=pl.ANY)
    smem = pl.BlockSpec(memory_space=pltpu.SMEM)

    def buf(k):
        return pltpu.VMEM((n, k, rows, w), F32)

    def pair(k):
        return pltpu.VMEM((n, k, 2, rows, w), F32)

    mixed, factor = pl.pallas_call(
        kernel,
        out_shape=(
            jax.ShapeDtypeStruct((3, 2, rows, columns), F32),
            jax.ShapeDtypeStruct((2, 8, LANES), F32),
        ),
        in_specs=[hbm, hbm, hbm, smem, smem],
        out_specs=(hbm, pl.BlockSpec(memory_space=pltpu.VMEM)),
        scratch_shapes=[
            pltpu.VMEM((n, rows, CHUNK), F32),
            buf(8), buf(5), buf(4), buf(3), buf(2), buf(5), buf(4), buf(3), buf(2),
            pair(8), pair(8), pair(8), pair(4),
            pltpu.VMEM((n, 2, rows, CHUNK), F32),
            pltpu.VMEM((5, 2, 8, LANES), F32), pltpu.VMEM((4, 2, 8, LANES), F32),
            pltpu.SemaphoreType.DMA((n,)), pltpu.SemaphoreType.DMA((n,)),
            pltpu.SemaphoreType.DMA((n, 17)), pltpu.SemaphoreType.DMA((n, 17)),
            pltpu.SemaphoreType.DMA((4,)), pltpu.SemaphoreType.DMA((4,)),
        ],
        compiler_params=pltpu.CompilerParams(
            collective_id=0, has_side_effects=True, vmem_limit_bytes=48 << 20),
        name="grow",
    )(old_weight, old_first, old_second, mixing, target_rms)
    scale = factor[:, :1, :1]
    return (scale * mixed[0], scale * mixed[1], scale * scale * mixed[2])


def solution(mesh):
    split = P("section", "tensor", None)
    return jax.shard_map(
        local,
        mesh=mesh,
        in_specs=(split, split, split, P(), P("section")),
        out_specs=(split, split, split),
        check_vma=False,
    )
```

```python
import jax
import jax.numpy as jnp
from jax import lax
from jax.experimental import pallas as pl
from jax.experimental.pallas import tpu as pltpu
from jax.sharding import PartitionSpec as P

MESH = pl.DeviceIdType.MESH
F32 = jnp.float32
PLANES = 8
LANES = 128

HUBS = 2
CHUNK = 1024
LEAD = 2
POW_LAG = 2
LAGS = (3, 6, 9, 12)


def plan(hubs):
    arm = (PLANES - hubs) // 2
    last = hubs - 1
    sizes = [hubs - s + arm for s in range(1, hubs + 1)]
    firsts = [(last + arm - (hubs - 2), hubs, 0, 1), (arm - 1, hubs, sizes[0] + arm - 1, -1)]
    for j in range(1, arm):
        firsts.append((last + arm + 1 + j, 1, hubs - 1 + j, 1 + j))
        firsts.append((arm - 1 - j, 1, sizes[0] + arm - 1 - j, -1 - j))
    passes = []
    for s in range(1, hubs):
        n = sizes[s]
        passes.append(((1, 0, n, 1), (sizes[s - 1], n, n, -1)))
    sources = []
    for h in range(hubs):
        found = [("own", last + arm - h, 0)]
        for s in range(1, h + 1):
            found.append((s - 1, last - h, -s))
        for j in range(arm):
            found.append((h, hubs - h - 1 + j, -(h + 1 + j)))
        for s in range(1, hubs - h):
            found.append((s - 1, sizes[s - 1] + arm + hubs - s - 1 - h, s))
        for j in range(arm):
            found.append((last - h, sizes[last - h] + arm - 1 - j, hubs + j - h))
        sources.append(found)
    targets = []
    for j in range(arm, -1, -1):
        targets += [(0, -j), (last, j)]
    targets += [(h, 0) for h in range(1, last)]
    finished = {}
    for place, (hub, step) in enumerate(targets):
        finished[(hub + step) % PLANES] = ("part" if step == 0 else "back", place)
    return arm, sizes, firsts, passes, sources, targets, finished


def kernel(weight, first, second, mixing_in, target_in, mixed, factor, mixing, target, found, stage, own, *rest):
    arm, sizes, firsts, passes, sources, targets, finished = plan(HUBS)
    rl, rest = rest[:HUBS], rest[HUBS:]
    (part, sent, came, back, done, pow_sent, pow_came,
     load_sem, out_sem, ssem, rsem, pow_ssem, pow_rsem) = rest
    count, _, rows, width = own.shape
    per = count // 3
    section = lax.axis_index("section")
    tensor = lax.axis_index("tensor")
    z = section // 2
    half = lax.rem(section, 2)

    def plane(step):
        return lax.rem(z + (step + PLANES), PLANES)

    def along(step):
        return (plane(step) * 2 + half, tensor)

    def flip(bit):
        return (section, tensor + bit - 2 * bit * lax.rem(tensor // bit, 2))

    across = (z * 2 + 1 - half, tensor)
    partners = [flip(bit) for bit in (1, 8, 2, 4)]

    loads = [pltpu.make_async_copy(array.at[0], stage.at[a], load_sem.at[a])
             for a, array in enumerate((weight, first, second))]
    loads.append(pltpu.make_async_copy(mixing_in, mixing, load_sem.at[3]))
    loads.append(pltpu.make_async_copy(target_in, target, load_sem.at[4]))
    for load in loads:
        load.start()

    barrier = pltpu.get_barrier_semaphore()
    peers = [along(way * step) for step in range(1, arm + 1) for way in (1, -1)] + [across] + partners
    for peer in peers:
        pl.semaphore_signal(barrier, inc=1, device_id=peer, device_id_type=MESH)
    for load in loads:
        load.wait()

    def remote(src, dst, c, k, device):
        return pltpu.make_async_remote_copy(
            src_ref=src, dst_ref=dst, send_sem=ssem.at[k], recv_sem=rsem.at[c, k],
            device_id=device, device_id_type=MESH)

    def landed(c, k, ref):
        pltpu.make_async_copy(ref.at[c], ref.at[c], rsem.at[c, k]).wait()

    def left(k, ref):
        pltpu.make_async_copy(ref, ref, ssem.at[k]).wait()

    def turn(c):
        a = c // per
        start = lax.rem(c, per) * CHUNK
        for i in range(PLANES):
            slab = plane(i - (HUBS + arm - 1))
            own[c, i] = stage[a, :, pl.ds(pl.multiple_of(start + slab * width, LANES), width)]

    def do_first(c):
        for at, n, to, step in firsts:
            remote(own.at[c, pl.ds(at, n)], rl[0].at[c, pl.ds(to, n)], c, 0, along(step)).start()

    def do_pass(s, c):
        landed(c, s - 1, rl[s - 1])
        for at, to, n, step in passes[s - 1]:
            remote(rl[s - 1].at[c, pl.ds(at, n)], rl[s].at[c, pl.ds(to, n)], c, s, along(step)).start()

    def mix(c, place):
        squared = c >= 2 * per
        hub, step = targets[place]
        to = plane(step) * 2
        coefs = []
        for _, _, away in sources[hub]:
            layer = plane(away) * 2 + half
            for new in (2 * (to + half), 2 * (to + 1 - half)):
                for n in range(2):
                    coef = mixing[layer, new + n]
                    coefs.append(coef * jnp.where(squared, coef, 1.0))
        for lane in range(0, width, LANES):
            lanes = pl.ds(lane, LANES)
            sums = [None] * 4
            for i, (name, at, _) in enumerate(sources[hub]):
                old = (own if name == "own" else rl[name])[c, at, :, lanes]
                for n in range(4):
                    term = coefs[4 * i + n] * old
                    sums[n] = term if i == 0 else sums[n] + term
            for n in range(2):
                part[c, place, n, :, lanes] = sums[n]
                sent[c, place, n, :, lanes] = sums[2 + n]

    def do_mix(c):
        landed(c, HUBS - 1, rl[HUBS - 1])
        for at in (0, 4):
            for place in range(at, at + 4):
                mix(c, place)
            remote(sent.at[c, pl.ds(at, 4)], came.at[c, pl.ds(at, 4)], c, HUBS, across).start()

    def do_join(c):
        landed(c, HUBS, came)
        for i in range(2 * arm):
            part[c, i] = part[c, i] + came[c, i]
            remote(part.at[c, i], back.at[c, i], c, HUBS + 1, along(targets[i][1])).start()
        for i in range(2 * arm, PLANES):
            part[c, i] = part[c, i] + came[c, i]

    def output(c):
        s = lax.rem(c, per)
        return pltpu.make_async_copy(
            done.at[c], mixed.at[c // per, :, :, pl.ds(pl.multiple_of(s * CHUNK, CHUNK), CHUNK)], out_sem.at[0])

    def power(c):
        for n in range(2):
            total = pow_sent[0, n]
            for lane in range(0, CHUNK, LANES):
                for row in range(0, rows, 8):
                    value = done[c, n, pl.ds(row, 8), pl.ds(lane, LANES)]
                    total = total + value * value
            pow_sent[0, n] = total

    def do_end(c):
        landed(c, HUBS + 1, back)
        for role in range(PLANES):
            slab = plane(-role)
            lanes = pl.ds(pl.multiple_of(slab * width, LANES), width)
            name, at = finished[role]
            done[c, :, :, lanes] = (part if name == "part" else back)[c, at]
        output(c).start()

        @pl.when(c < per)
        def _():
            power(c)

    def pow_copy(k):
        return pltpu.make_async_remote_copy(
            src_ref=pow_sent.at[k], dst_ref=pow_came.at[k], send_sem=pow_ssem.at[k], recv_sem=pow_rsem.at[k],
            device_id=partners[k], device_id_type=MESH)

    factor_copy = pltpu.make_async_copy(found, factor, load_sem.at[5])

    def do_factor():
        total_count = rows * lax.axis_size("tensor") * CHUNK * per
        for n in range(2):
            total = jnp.sum(pow_sent[len(partners), n], keepdims=True)
            value = 1.0 / jnp.sqrt(total / total_count + 1e-06)
            scale = target[n] * value[0, 0]
            found[0, n] = scale
            found[1, n] = scale * scale
        factor_copy.start()

    pow_sent[0] = jnp.zeros_like(pow_sent[0])
    for c in range(LEAD):
        turn(c)
    pl.semaphore_wait(barrier, len(peers))
    for c in range(LEAD):
        do_first(c)

    pow_turn = LAGS[-1] + per - 1
    turns = max(count + LAGS[-1], pow_turn + POW_LAG * len(partners) + 1)

    def do_start(c):
        turn(c)
        do_first(c)

    steps = [(-LEAD, do_start)]
    for s in range(1, HUBS):
        steps.append((LAGS[s - 1], lambda c, s=s: do_pass(s, c)))
    steps += [(LAGS[-2], do_join), (LAGS[-1], do_end), (LAGS[-3], do_mix)]

    def turn_of(t, _):
        for lag, step in steps:
            c = t - lag

            @pl.when((c >= 0) & (c < count))
            def _(c=c, step=step):
                step(c)

        for k in range(len(partners) + 1):
            @pl.when(t == pow_turn + POW_LAG * k)
            def _(k=k):
                if k > 0:
                    pow_copy(k - 1).wait()
                    pow_sent[k] = pow_sent[k - 1] + pow_came[k - 1]
                if k < len(partners):
                    pow_copy(k).start()
                else:
                    do_factor()
        return 0

    lax.fori_loop(0, turns, turn_of, 0)

    for k, ref in enumerate((*rl, came, back)):
        left(k, ref)
    pltpu.make_async_copy(done, done, out_sem.at[0]).wait()
    factor_copy.wait()


def local(old_weight, old_first, old_second, mixing, target_rms):
    rows, columns = old_weight.shape[1:]
    n = 3 * columns // CHUNK
    w = CHUNK // PLANES
    arm, sizes = plan(HUBS)[:2]
    hbm = pl.BlockSpec(memory_space=pltpu.HBM)
    dma = pltpu.SemaphoreType.DMA

    def buf(k):
        return pltpu.VMEM((n, k, rows, w), F32)

    def pair(k):
        return pltpu.VMEM((n, k, 2, rows, w), F32)

    mixed, factor = pl.pallas_call(
        kernel,
        out_shape=(
            jax.ShapeDtypeStruct((3, 2, rows, columns), F32),
            jax.ShapeDtypeStruct((2, 2), F32),
        ),
        in_specs=[hbm] * 5,
        out_specs=(pl.BlockSpec(memory_space=pl.ANY), pl.BlockSpec(memory_space=pl.ANY)),
        scratch_shapes=[
            pltpu.SMEM(mixing.shape[::-1], F32), pltpu.SMEM(target_rms.shape, F32), pltpu.SMEM((2, 2), F32),
            pltpu.VMEM((3, rows, columns), F32), buf(PLANES), *[buf(2 * size) for size in sizes],
            pair(PLANES), pair(PLANES), pair(PLANES), pair(2 * arm),
            pltpu.VMEM((n, 2, rows, CHUNK), F32),
            pltpu.VMEM((5, 2, 8, LANES), F32), pltpu.VMEM((4, 2, 8, LANES), F32),
            dma((6,)), dma((1,)), dma((HUBS + 2,)), dma((n, HUBS + 2)), dma((4,)), dma((4,)),
        ],
        compiler_params=pltpu.CompilerParams(
            collective_id=0, has_side_effects=True, vmem_limit_bytes=60 << 20),
        name="grow",
    )(old_weight, old_first, old_second, mixing.T, target_rms)
    scale = factor[0][:, None, None]
    square = factor[1][:, None, None]
    return (scale * mixed[0], scale * mixed[1], square * mixed[2])


def solution(mesh):
    split = P("section", "tensor", None)
    return jax.shard_map(
        local,
        mesh=mesh,
        in_specs=(split, split, split, P(), P("section")),
        out_specs=(split, split, split),
        check_vma=False,
    )
```

```python
import jax
import jax.numpy as jnp
from jax import lax
from jax.experimental import pallas as pl
from jax.experimental.pallas import tpu as pltpu
from jax.sharding import PartitionSpec as P

MESH = pl.DeviceIdType.MESH
F32 = jnp.float32
PLANES = 8
LANES = 128

GROUPS = ((2, 1024, 18, 0, (3, 6, 9, 12)),)
ORDER = ("first", "pass", "join", "end", "mix")
LEAD = 2
POW_LAG = 2


def plan(hubs):
    arm = (PLANES - hubs) // 2
    last = hubs - 1
    sizes = [hubs - s + arm for s in range(1, hubs + 1)]
    firsts = [(last + arm - (hubs - 2), hubs, 0, 1), (arm - 1, hubs, sizes[0] + arm - 1, -1)]
    for j in range(1, arm):
        firsts.append((last + arm + 1 + j, 1, hubs - 1 + j, 1 + j))
        firsts.append((arm - 1 - j, 1, sizes[0] + arm - 1 - j, -1 - j))
    passes = []
    for s in range(1, hubs):
        n = sizes[s]
        passes.append(((1, 0, n, 1), (sizes[s - 1], n, n, -1)))
    sources = []
    for h in range(hubs):
        found = [("own", last + arm - h, 0)]
        for s in range(1, h + 1):
            found.append((s - 1, last - h, -s))
        for j in range(arm):
            found.append((h, hubs - h - 1 + j, -(h + 1 + j)))
        for s in range(1, hubs - h):
            found.append((s - 1, sizes[s - 1] + arm + hubs - s - 1 - h, s))
        for j in range(arm):
            found.append((last - h, sizes[last - h] + arm - 1 - j, hubs + j - h))
        sources.append(found)
    targets = []
    for j in range(arm, -1, -1):
        targets += [(0, -j), (last, j)]
    targets += [(h, 0) for h in range(1, last)]
    finished = {}
    for place, (hub, step) in enumerate(targets):
        finished[(hub + step) % PLANES] = ("part" if step == 0 else "back", place)
    return arm, sizes, firsts, passes, sources, targets, finished


class Group:
    def __init__(self, spec, start, columns, refs, sems):
        self.hubs, self.chunk, self.count, self.base, self.lags = spec
        self.start, self.columns = start, columns
        self.width = self.chunk // PLANES
        (self.arm, self.sizes, self.firsts, self.passes, self.sources, self.targets,
         self.finished) = plan(self.hubs)
        self.own, self.part, self.sent, self.came, self.back, *self.rl = refs
        self.ssem, self.rsem = sems

    def where(self, c):
        at = self.start + c * self.chunk
        return at // self.columns, pl.multiple_of(lax.rem(at, self.columns), LANES)

    def landed(self, c, k, ref):
        pltpu.make_async_copy(ref.at[c], ref.at[c], self.rsem.at[c, k]).wait()


def kernel(*refs):
    (weight, first, second, mixing_in, target_in, mixed, factor, mixing, target, found,
     stage, done, pow_sent, pow_came, load_sem, out_sem, pow_ssem, pow_rsem), refs = refs[:18], refs[18:]
    _, rows, columns = stage.shape
    groups = []
    start = 0
    for spec in GROUPS:
        n = 5 + spec[0]
        groups.append(Group(spec, start, columns, refs[:n], refs[n:n + 2]))
        refs = refs[n + 2:]
        start += spec[1] * spec[2]
    section = lax.axis_index("section")
    tensor = lax.axis_index("tensor")
    z = section // 2
    half = lax.rem(section, 2)

    def plane(step):
        return lax.rem(z + (step + PLANES), PLANES)

    def along(step):
        return (plane(step) * 2 + half, tensor)

    def flip(bit):
        return (section, tensor + bit - 2 * bit * lax.rem(tensor // bit, 2))

    across = (z * 2 + 1 - half, tensor)
    partners = [flip(bit) for bit in (1, 8, 2, 4)]

    loads = [pltpu.make_async_copy(array.at[0], stage.at[a], load_sem.at[a])
             for a, array in enumerate((weight, first, second))]
    loads.append(pltpu.make_async_copy(mixing_in, mixing, load_sem.at[3]))
    loads.append(pltpu.make_async_copy(target_in, target, load_sem.at[4]))
    for load in loads:
        load.start()

    barrier = pltpu.get_barrier_semaphore()
    reach = max(group.arm for group in groups)
    peers = [along(way * step) for step in range(1, reach + 1) for way in (1, -1)] + [across] + partners
    for peer in peers:
        pl.semaphore_signal(barrier, inc=1, device_id=peer, device_id_type=MESH)

    def remote(g, src, dst, c, k, device):
        return pltpu.make_async_remote_copy(
            src_ref=src, dst_ref=dst, send_sem=g.ssem.at[k], recv_sem=g.rsem.at[c, k],
            device_id=device, device_id_type=MESH)

    def turn(g, c):
        a, col = g.where(c)
        for i in range(PLANES):
            slab = plane(i - (g.hubs + g.arm - 1))
            g.own[c, i] = stage[a, :, pl.ds(pl.multiple_of(col + slab * g.width, LANES), g.width)]

    def do_first(g, c):
        for at, n, to, step in g.firsts:
            remote(g, g.own.at[c, pl.ds(at, n)], g.rl[0].at[c, pl.ds(to, n)], c, 0, along(step)).start()

    def do_start(g, c):
        turn(g, c)
        do_first(g, c)

    def do_pass(s, g, c):
        g.landed(c, s - 1, g.rl[s - 1])
        for at, to, n, step in g.passes[s - 1]:
            remote(g, g.rl[s - 1].at[c, pl.ds(at, n)], g.rl[s].at[c, pl.ds(to, n)], c, s, along(step)).start()

    def mix(g, c, place):
        squared = g.where(c)[0] == 2
        hub, step = g.targets[place]
        to = plane(step) * 2
        coefs = []
        for _, _, away in g.sources[hub]:
            layer = plane(away) * 2 + half
            for new in (2 * (to + half), 2 * (to + 1 - half)):
                for n in range(2):
                    coef = mixing[layer, new + n]
                    coefs.append(coef * jnp.where(squared, coef, 1.0))
        for lane in range(0, g.width, LANES):
            lanes = pl.ds(lane, LANES)
            sums = [None] * 4
            for i, (name, at, _) in enumerate(g.sources[hub]):
                old = (g.own if name == "own" else g.rl[name])[c, at, :, lanes]
                for n in range(4):
                    term = coefs[4 * i + n] * old
                    sums[n] = term if i == 0 else sums[n] + term
            for n in range(2):
                g.part[c, place, n, :, lanes] = sums[n]
                g.sent[c, place, n, :, lanes] = sums[2 + n]

    def do_mix(g, c):
        g.landed(c, g.hubs - 1, g.rl[g.hubs - 1])
        for at in (0, 4):
            for place in range(at, at + 4):
                mix(g, c, place)
            remote(g, g.sent.at[c, pl.ds(at, 4)], g.came.at[c, pl.ds(at, 4)], c, g.hubs, across).start()

    def do_join(g, c):
        g.landed(c, g.hubs, g.came)
        for i in range(2 * g.arm):
            g.part[c, i] = g.part[c, i] + g.came[c, i]
            remote(g, g.part.at[c, i], g.back.at[c, i], c, g.hubs + 1, along(g.targets[i][1])).start()
        for i in range(2 * g.arm, PLANES):
            g.part[c, i] = g.part[c, i] + g.came[c, i]

    def do_end(g, c):
        g.landed(c, g.hubs + 1, g.back)
        a, col = g.where(c)
        for role in range(PLANES):
            slab = plane(-role)
            lanes = pl.ds(pl.multiple_of(col + slab * g.width, LANES), g.width)
            name, at = g.finished[role]
            done[a, :, :, lanes] = (g.part if name == "part" else g.back)[c, at]
        lanes = pl.ds(col, g.chunk)
        pltpu.make_async_copy(done.at[a, :, :, lanes], mixed.at[a, :, :, lanes], out_sem.at[0]).start()

        @pl.when(a == 0)
        def _():
            for n in range(2):
                total = pow_sent[0, n]
                for lane in range(0, g.chunk, LANES):
                    for row in range(0, rows, 8):
                        value = done[0, n, pl.ds(row, 8), pl.ds(pl.multiple_of(col + lane, LANES), LANES)]
                        total = total + value * value
                pow_sent[0, n] = total

    def pow_copy(k):
        return pltpu.make_async_remote_copy(
            src_ref=pow_sent.at[k], dst_ref=pow_came.at[k], send_sem=pow_ssem.at[k], recv_sem=pow_rsem.at[k],
            device_id=partners[k], device_id_type=MESH)

    factor_copy = pltpu.make_async_copy(found, factor, load_sem.at[5])

    def do_factor():
        total_count = rows * lax.axis_size("tensor") * columns
        for n in range(2):
            total = jnp.sum(pow_sent[len(partners), n], keepdims=True)
            value = 1.0 / jnp.sqrt(total / total_count + 1e-06)
            scale = target[n] * value[0, 0]
            found[0, n] = scale
            found[1, n] = scale * scale
        factor_copy.start()

    pow_sent[0] = jnp.zeros_like(pow_sent[0])
    loads[0].wait()
    for c in range(LEAD):
        turn(groups[0], c)
    pl.semaphore_wait(barrier, len(peers))
    for c in range(LEAD):
        do_first(groups[0], c)
    for load in loads[1:]:
        load.wait()

    steps = []
    for kind in ORDER:
        for i, g in enumerate(groups):
            if kind == "first":
                steps.append((g, g.base - LEAD, 0 if i else LEAD, do_start))
            elif kind == "pass":
                for s in range(1, g.hubs):
                    steps.append((g, g.base + g.lags[s - 1], 0, lambda g, c, s=s: do_pass(s, g, c)))
            else:
                at, step = {"mix": (-3, do_mix), "join": (-2, do_join), "end": (-1, do_end)}[kind]
                steps.append((g, g.base + g.lags[at], 0, step))
    pow_turn = max(g.base + g.lags[-1] + min(g.count, (columns - g.start) // g.chunk) - 1
                   for g in groups if g.start < columns)
    turns = max([g.base + g.lags[-1] + g.count for g in groups] + [pow_turn + POW_LAG * len(partners) + 1])

    def turn_of(t, _):
        for g, lag, least, step in steps:
            c = t - lag

            @pl.when((c >= least) & (c < g.count))
            def _(g=g, c=c, step=step):
                step(g, c)

        for k in range(len(partners) + 1):
            @pl.when(t == pow_turn + POW_LAG * k)
            def _(k=k):
                if k > 0:
                    pow_copy(k - 1).wait()
                    pow_sent[k] = pow_sent[k - 1] + pow_came[k - 1]
                if k < len(partners):
                    pow_copy(k).start()
                else:
                    do_factor()
        return 0

    lax.fori_loop(0, turns, turn_of, 0)

    for g in groups:
        for k, ref in enumerate((*g.rl, g.came, g.back)):
            pltpu.make_async_copy(ref, ref, g.ssem.at[k]).wait()
    pltpu.make_async_copy(done, done, out_sem.at[0]).wait()
    factor_copy.wait()


def scaled(factor_in, mixed, new_weight, new_first, new_second, factor, held, factor_sem, in_sem, out_sem):
    factor_copy = pltpu.make_async_copy(factor_in, factor, factor_sem.at[0])
    factor_copy.start()
    parts = [(a, n) for a in range(3) for n in range(2)]
    for a, n in parts:
        pltpu.make_async_copy(mixed.at[a, n], held.at[a, n], in_sem.at[a, n]).start()
    factor_copy.wait()
    outs = (new_weight, new_first, new_second)
    for a, n in parts:
        pltpu.make_async_copy(mixed.at[a, n], held.at[a, n], in_sem.at[a, n]).wait()
        scale = factor[1 if a == 2 else 0, n]
        held[a, n] = held[a, n] * scale
        pltpu.make_async_copy(held.at[a, n], outs[a].at[n], out_sem.at[a, n]).start()
    for a, n in parts:
        pltpu.make_async_copy(held.at[a, n], outs[a].at[n], out_sem.at[a, n]).wait()


def local(old_weight, old_first, old_second, mixing, target_rms):
    rows, columns = old_weight.shape[1:]
    hbm = pl.BlockSpec(memory_space=pltpu.HBM)
    dma = pltpu.SemaphoreType.DMA
    scratch = []
    for hubs, chunk, n, _, _ in GROUPS:
        arm, sizes = plan(hubs)[:2]
        w = chunk // PLANES
        for k in (PLANES,):
            scratch.append(pltpu.VMEM((n, k, rows, w), F32))
        for k in (PLANES, PLANES, PLANES, 2 * arm):
            scratch.append(pltpu.VMEM((n, k, 2, rows, w), F32))
        for size in sizes:
            scratch.append(pltpu.VMEM((n, 2 * size, rows, w), F32))
        scratch += [dma((hubs + 2,)), dma((n, hubs + 2))]
    mixed, factor = pl.pallas_call(
        kernel,
        out_shape=(
            jax.ShapeDtypeStruct((3, 2, rows, columns), F32),
            jax.ShapeDtypeStruct((2, 2), F32),
        ),
        in_specs=[hbm] * 5,
        out_specs=(hbm, hbm),
        scratch_shapes=[
            pltpu.SMEM(mixing.shape[::-1], F32), pltpu.SMEM(target_rms.shape, F32), pltpu.SMEM((2, 2), F32),
            pltpu.VMEM((3, rows, columns), F32), pltpu.VMEM((3, 2, rows, columns), F32),
            pltpu.VMEM((5, 2, 8, LANES), F32), pltpu.VMEM((4, 2, 8, LANES), F32),
            dma((6,)), dma((1,)), dma((4,)), dma((4,)), *scratch,
        ],
        compiler_params=pltpu.CompilerParams(
            collective_id=0, has_side_effects=True, vmem_limit_bytes=60 << 20),
        name="grow",
    )(old_weight, old_first, old_second, mixing.T, target_rms)
    new = jax.ShapeDtypeStruct((2, rows, columns), F32)
    return pl.pallas_call(
        scaled,
        out_shape=(new, new, new),
        in_specs=[hbm, hbm],
        out_specs=(hbm, hbm, hbm),
        scratch_shapes=[
            pltpu.SMEM((2, 2), F32), pltpu.VMEM((3, 2, rows, columns), F32),
            dma((1,)), dma((3, 2)), dma((3, 2)),
        ],
        compiler_params=pltpu.CompilerParams(vmem_limit_bytes=60 << 20),
        name="scale",
    )(factor, mixed)


def solution(mesh):
    split = P("section", "tensor", None)
    return jax.shard_map(
        local,
        mesh=mesh,
        in_specs=(split, split, split, P(), P("section")),
        out_specs=(split, split, split),
        check_vma=False,
    )
```

```python
import jax
import jax.numpy as jnp
from jax import lax
from jax.experimental import pallas as pl
from jax.experimental.pallas import tpu as pltpu
from jax.sharding import PartitionSpec as P

MESH = pl.DeviceIdType.MESH
F32 = jnp.float32
PLANES = 8
LANES = 128

GROUPS = (
    (2, 3, 1024, 16, 0, (3, 6, 9, 12), 1),
    (4, 2, 1024, 2, 0, (3, 6, 9, 12, 15, 18), 5),
)
ORDER = ("first", "pass", "join", "end", "mix")
LEAD = 2
POW_LAG = 2


def plan(hubs, before):
    after = PLANES - hubs - before
    last = hubs - 1
    right = [hubs - s + before for s in range(1, hubs + 1)]
    left = [hubs - s + after for s in range(1, hubs + 1)]
    firsts = [(after + 1, hubs, 0, 1), (after - 1, hubs, right[0] + after - 1, -1)]
    for j in range(1, max(before, after)):
        if j < before:
            firsts.append((hubs + after + j, 1, last + j, 1 + j))
        if j < after:
            firsts.append((after - 1 - j, 1, right[0] + after - 1 - j, -1 - j))
    passes = [((1, 0, right[s], 1), (right[s - 1], right[s], left[s], -1)) for s in range(1, hubs)]
    sources = []
    for h in range(hubs):
        found = [("own", last + after - h, 0)]
        for s in range(1, h + 1):
            found.append((s - 1, last - h, -s))
        for j in range(before):
            found.append((h, last - h + j, -(h + 1 + j)))
        for s in range(1, hubs - h):
            found.append((s - 1, right[s - 1] + after + last - s - h, s))
        for j in range(after):
            found.append((last - h, right[last - h] + after - 1 - j, hubs + j - h))
        sources.append(found)
    targets = []
    for j in range(max(before, after), 0, -1):
        targets += [(0, -j)] * (j <= before) + [(last, j)] * (j <= after)
    targets += [(0, 0), (last, 0)] + [(h, 0) for h in range(1, last)]
    finished = {}
    for place, (hub, step) in enumerate(targets):
        finished[(hub + step) % PLANES] = ("part" if step == 0 else "back", place)
    sizes = [r + l for r, l in zip(right, left)]
    return sizes, firsts, passes, sources, targets, finished


class Group:
    def __init__(self, spec, start, columns, refs, sems):
        self.hubs, self.before, self.chunk, self.count, self.base, self.lags, self.stride = spec
        self.arms = PLANES - self.hubs
        self.after = self.arms - self.before
        self.start, self.columns = start, columns
        self.width = self.chunk // PLANES
        (_, self.firsts, self.passes, self.sources, self.targets,
         self.finished) = plan(self.hubs, self.before)
        self.own, self.part, self.sent, self.came, self.back, *self.rl = refs
        self.ssem, self.rsem = sems

    def where(self, c):
        at = self.start + c * self.chunk
        return at // self.columns, pl.multiple_of(lax.rem(at, self.columns), LANES)

    def landed(self, c, k, ref):
        pltpu.make_async_copy(ref.at[c], ref.at[c], self.rsem.at[c, k]).wait()


def kernel(*refs):
    (weight, first, second, mixing_in, target_in, mixed, factor, mixing, target, found,
     stage, done, pow_sent, pow_came, load_sem, out_sem, pow_ssem, pow_rsem), refs = refs[:18], refs[18:]
    _, rows, columns = stage.shape
    groups = []
    start = 0
    for spec in GROUPS:
        n = 5 + spec[0]
        groups.append(Group(spec, start, columns, refs[:n], refs[n:n + 2]))
        refs = refs[n + 2:]
        start += spec[2] * spec[3]
    section = lax.axis_index("section")
    tensor = lax.axis_index("tensor")
    z = section // 2
    half = lax.rem(section, 2)

    def plane(step):
        return lax.rem(z + (step + PLANES), PLANES)

    def along(step):
        return (plane(step) * 2 + half, tensor)

    def flip(bit):
        return (section, tensor + bit - 2 * bit * lax.rem(tensor // bit, 2))

    across = (z * 2 + 1 - half, tensor)
    partners = [flip(bit) for bit in (1, 8, 2, 4)]

    loads = [pltpu.make_async_copy(array.at[0], stage.at[a], load_sem.at[a])
             for a, array in enumerate((weight, first, second))]
    loads.append(pltpu.make_async_copy(mixing_in, mixing, load_sem.at[3]))
    loads.append(pltpu.make_async_copy(target_in, target, load_sem.at[4]))
    for load in loads:
        load.start()

    barrier = pltpu.get_barrier_semaphore()
    reach = max(max(group.before, group.after) for group in groups)
    peers = [along(way * step) for step in range(1, reach + 1) for way in (1, -1)] + [across] + partners
    for peer in peers:
        pl.semaphore_signal(barrier, inc=1, device_id=peer, device_id_type=MESH)

    def remote(g, src, dst, c, k, device):
        return pltpu.make_async_remote_copy(
            src_ref=src, dst_ref=dst, send_sem=g.ssem.at[k], recv_sem=g.rsem.at[c, k],
            device_id=device, device_id_type=MESH)

    def turn(g, c):
        a, col = g.where(c)
        for i in range(PLANES):
            slab = plane(i - (g.hubs + g.after - 1))
            g.own[c, i] = stage[a, :, pl.ds(pl.multiple_of(col + slab * g.width, LANES), g.width)]

    def do_first(g, c):
        for at, n, to, step in g.firsts:
            remote(g, g.own.at[c, pl.ds(at, n)], g.rl[0].at[c, pl.ds(to, n)], c, 0, along(step)).start()

    def do_start(g, c):
        turn(g, c)
        do_first(g, c)

    def do_pass(s, g, c):
        g.landed(c, s - 1, g.rl[s - 1])
        for at, to, n, step in g.passes[s - 1]:
            remote(g, g.rl[s - 1].at[c, pl.ds(at, n)], g.rl[s].at[c, pl.ds(to, n)], c, s, along(step)).start()

    def mix(g, c, place):
        squared = g.where(c)[0] == 2
        hub, step = g.targets[place]
        to = plane(step) * 2
        coefs = []
        for _, _, away in g.sources[hub]:
            layer = plane(away) * 2 + half
            for new in (2 * (to + half), 2 * (to + 1 - half)):
                for n in range(2):
                    coef = mixing[layer, new + n]
                    coefs.append(coef * jnp.where(squared, coef, 1.0))
        for lane in range(0, g.width, LANES):
            lanes = pl.ds(lane, LANES)
            sums = [None] * 4
            for i, (name, at, _) in enumerate(g.sources[hub]):
                old = (g.own if name == "own" else g.rl[name])[c, at, :, lanes]
                for n in range(4):
                    term = coefs[4 * i + n] * old
                    sums[n] = term if i == 0 else sums[n] + term
            for n in range(2):
                g.part[c, place, n, :, lanes] = sums[n]
                g.sent[c, place, n, :, lanes] = sums[2 + n]

    def do_mix(g, c):
        g.landed(c, g.hubs - 1, g.rl[g.hubs - 1])
        for at in (0, 4):
            for place in range(at, at + 4):
                mix(g, c, place)
            remote(g, g.sent.at[c, pl.ds(at, 4)], g.came.at[c, pl.ds(at, 4)], c, g.hubs, across).start()

    def do_join(g, c):
        g.landed(c, g.hubs, g.came)
        for i in range(g.arms):
            g.part[c, i] = g.part[c, i] + g.came[c, i]
            remote(g, g.part.at[c, i], g.back.at[c, i], c, g.hubs + 1, along(g.targets[i][1])).start()
        for i in range(g.arms, PLANES):
            g.part[c, i] = g.part[c, i] + g.came[c, i]

    def do_end(g, c):
        g.landed(c, g.hubs + 1, g.back)
        a, col = g.where(c)
        for role in range(PLANES):
            slab = plane(-role)
            lanes = pl.ds(pl.multiple_of(col + slab * g.width, LANES), g.width)
            name, at = g.finished[role]
            done[a, :, :, lanes] = (g.part if name == "part" else g.back)[c, at]
        lanes = pl.ds(col, g.chunk)
        pltpu.make_async_copy(done.at[a, :, :, lanes], mixed.at[a, :, :, lanes], out_sem.at[0]).start()

        @pl.when(a == 0)
        def _():
            for n in range(2):
                total = pow_sent[0, n]
                for lane in range(0, g.chunk, LANES):
                    for row in range(0, rows, 8):
                        value = done[0, n, pl.ds(row, 8), pl.ds(pl.multiple_of(col + lane, LANES), LANES)]
                        total = total + value * value
                pow_sent[0, n] = total

    def pow_copy(k):
        return pltpu.make_async_remote_copy(
            src_ref=pow_sent.at[k], dst_ref=pow_came.at[k], send_sem=pow_ssem.at[k], recv_sem=pow_rsem.at[k],
            device_id=partners[k], device_id_type=MESH)

    factor_copy = pltpu.make_async_copy(found, factor, load_sem.at[5])

    def do_factor():
        total_count = rows * lax.axis_size("tensor") * columns
        for n in range(2):
            total = jnp.sum(pow_sent[len(partners), n], keepdims=True)
            value = 1.0 / jnp.sqrt(total / total_count + 1e-06)
            scale = target[n] * value[0, 0]
            found[0, n] = scale
            found[1, n] = scale * scale
        factor_copy.start()

    pow_sent[0] = jnp.zeros_like(pow_sent[0])
    loads[0].wait()
    for c in range(LEAD):
        turn(groups[0], c)
    pl.semaphore_wait(barrier, len(peers))
    for c in range(LEAD):
        do_first(groups[0], c)
    for load in loads[1:]:
        load.wait()

    steps = []
    for kind in ORDER:
        for i, g in enumerate(groups):
            if kind == "first":
                steps.append((g, g.base - (0 if i else LEAD) * g.stride, 0 if i else LEAD, do_start))
            elif kind == "pass":
                for s in range(1, g.hubs):
                    steps.append((g, g.base + g.lags[s - 1], 0, lambda g, c, s=s: do_pass(s, g, c)))
            else:
                at, step = {"mix": (-3, do_mix), "join": (-2, do_join), "end": (-1, do_end)}[kind]
                steps.append((g, g.base + g.lags[at], 0, step))
    pow_turn = max(g.base + g.lags[-1] + (min(g.count, (columns - g.start) // g.chunk) - 1) * g.stride
                   for g in groups if g.start < columns)
    turns = max([g.base + g.lags[-1] + (g.count - 1) * g.stride + 1 for g in groups] + [pow_turn + POW_LAG * len(partners) + 1])

    def turn_of(t, _):
        for g, lag, least, step in steps:
            c = (t - lag) // g.stride if g.stride > 1 else t - lag
            on_turn = (t - lag >= 0) & (c >= least) & (c < g.count)
            if g.stride > 1:
                on_turn &= lax.rem(t - lag, g.stride) == 0

            @pl.when(on_turn)
            def _(g=g, c=c, step=step):
                step(g, c)

        for k in range(len(partners) + 1):
            @pl.when(t == pow_turn + POW_LAG * k)
            def _(k=k):
                if k > 0:
                    pow_copy(k - 1).wait()
                    pow_sent[k] = pow_sent[k - 1] + pow_came[k - 1]
                if k < len(partners):
                    pow_copy(k).start()
                else:
                    do_factor()
        return 0

    lax.fori_loop(0, turns, turn_of, 0)

    for g in groups:
        for k, ref in enumerate((*g.rl, g.came, g.back)):
            pltpu.make_async_copy(ref, ref, g.ssem.at[k]).wait()
    pltpu.make_async_copy(done, done, out_sem.at[0]).wait()
    factor_copy.wait()


def scaled(factor_in, mixed, new_weight, new_first, new_second, factor, held, factor_sem, in_sem, out_sem):
    factor_copy = pltpu.make_async_copy(factor_in, factor, factor_sem.at[0])
    factor_copy.start()
    parts = [(a, n) for a in range(3) for n in range(2)]
    for a, n in parts:
        pltpu.make_async_copy(mixed.at[a, n], held.at[a, n], in_sem.at[a, n]).start()
    factor_copy.wait()
    outs = (new_weight, new_first, new_second)
    for a, n in parts:
        pltpu.make_async_copy(mixed.at[a, n], held.at[a, n], in_sem.at[a, n]).wait()
        scale = factor[1 if a == 2 else 0, n]
        held[a, n] = held[a, n] * scale
        pltpu.make_async_copy(held.at[a, n], outs[a].at[n], out_sem.at[a, n]).start()
    for a, n in parts:
        pltpu.make_async_copy(held.at[a, n], outs[a].at[n], out_sem.at[a, n]).wait()


def local(old_weight, old_first, old_second, mixing, target_rms):
    rows, columns = old_weight.shape[1:]
    hbm = pl.BlockSpec(memory_space=pltpu.HBM)
    dma = pltpu.SemaphoreType.DMA
    scratch = []
    for hubs, before, chunk, n, _, _, _ in GROUPS:
        sizes = plan(hubs, before)[0]
        w = chunk // PLANES
        for k in (PLANES,):
            scratch.append(pltpu.VMEM((n, k, rows, w), F32))
        for k in (PLANES, PLANES, PLANES, PLANES - hubs):
            scratch.append(pltpu.VMEM((n, k, 2, rows, w), F32))
        for size in sizes:
            scratch.append(pltpu.VMEM((n, size, rows, w), F32))
        scratch += [dma((hubs + 2,)), dma((n, hubs + 2))]
    mixed, factor = pl.pallas_call(
        kernel,
        out_shape=(
            jax.ShapeDtypeStruct((3, 2, rows, columns), F32),
            jax.ShapeDtypeStruct((2, 2), F32),
        ),
        in_specs=[hbm] * 5,
        out_specs=(hbm, hbm),
        scratch_shapes=[
            pltpu.SMEM(mixing.shape[::-1], F32), pltpu.SMEM(target_rms.shape, F32), pltpu.SMEM((2, 2), F32),
            pltpu.VMEM((3, rows, columns), F32), pltpu.VMEM((3, 2, rows, columns), F32),
            pltpu.VMEM((5, 2, 8, LANES), F32), pltpu.VMEM((4, 2, 8, LANES), F32),
            dma((6,)), dma((1,)), dma((4,)), dma((4,)), *scratch,
        ],
        compiler_params=pltpu.CompilerParams(
            collective_id=0, has_side_effects=True, vmem_limit_bytes=60 << 20),
        name="grow",
    )(old_weight, old_first, old_second, mixing.T, target_rms)
    new = jax.ShapeDtypeStruct((2, rows, columns), F32)
    return pl.pallas_call(
        scaled,
        out_shape=(new, new, new),
        in_specs=[hbm, hbm],
        out_specs=(hbm, hbm, hbm),
        scratch_shapes=[
            pltpu.SMEM((2, 2), F32), pltpu.VMEM((3, 2, rows, columns), F32),
            dma((1,)), dma((3, 2)), dma((3, 2)),
        ],
        compiler_params=pltpu.CompilerParams(vmem_limit_bytes=60 << 20),
        name="scale",
    )(factor, mixed)


def solution(mesh):
    split = P("section", "tensor", None)
    return jax.shard_map(
        local,
        mesh=mesh,
        in_specs=(split, split, split, P(), P("section")),
        out_specs=(split, split, split),
        check_vma=False,
    )
```

```python
import jax
import jax.numpy as jnp
from jax import lax
from jax.experimental import pallas as pl
from jax.experimental.pallas import tpu as pltpu
from jax.sharding import PartitionSpec as P

MESH = pl.DeviceIdType.MESH
F32 = jnp.float32
PLANES = 8
LANES = 128

GROUPS = (
    (2, 3, 1024, 16, 0, (3, 6, 9, 12), 1),
    (4, 2, 1024, 2, 0, (3, 6, 9, 12, 15, 18), 5),
)
ORDER = ("first", "pass", "join", "end", "mix")
LEAD = 2
POW_LAG = 2


def plan(hubs, before):
    after = PLANES - hubs - before
    last = hubs - 1
    right = [hubs - s + before for s in range(1, hubs + 1)]
    left = [hubs - s + after for s in range(1, hubs + 1)]
    firsts = [(after + 1, hubs, 0, 1), (after - 1, hubs, right[0] + after - 1, -1)]
    for j in range(1, max(before, after)):
        if j < before:
            firsts.append((hubs + after + j, 1, last + j, 1 + j))
        if j < after:
            firsts.append((after - 1 - j, 1, right[0] + after - 1 - j, -1 - j))
    passes = [((1, 0, right[s], 1), (right[s - 1], right[s], left[s], -1)) for s in range(1, hubs)]
    sources = []
    for h in range(hubs):
        found = [("own", last + after - h, 0)]
        for s in range(1, h + 1):
            found.append((s - 1, last - h, -s))
        for j in range(before):
            found.append((h, last - h + j, -(h + 1 + j)))
        for s in range(1, hubs - h):
            found.append((s - 1, right[s - 1] + after + last - s - h, s))
        for j in range(after):
            found.append((last - h, right[last - h] + after - 1 - j, hubs + j - h))
        sources.append(found)
    targets = []
    for j in range(max(before, after), 0, -1):
        targets += [(0, -j)] * (j <= before) + [(last, j)] * (j <= after)
    targets += [(0, 0), (last, 0)] + [(h, 0) for h in range(1, last)]
    finished = {}
    for place, (hub, step) in enumerate(targets):
        finished[(hub + step) % PLANES] = ("part" if step == 0 else "back", place)
    sizes = [r + l for r, l in zip(right, left)]
    return sizes, firsts, passes, sources, targets, finished


class Group:
    def __init__(self, spec, start, columns, refs, sems):
        self.hubs, self.before, self.chunk, self.count, self.base, self.lags, self.stride = spec
        self.arms = PLANES - self.hubs
        self.after = self.arms - self.before
        self.start, self.columns = start, columns
        self.width = self.chunk // PLANES
        (_, self.firsts, self.passes, self.sources, self.targets,
         self.finished) = plan(self.hubs, self.before)
        self.own, self.part, self.sent, self.came, self.back, *self.rl = refs
        self.ssem, self.rsem = sems

    def where(self, c):
        at = self.start + c * self.chunk
        return at // self.columns, pl.multiple_of(lax.rem(at, self.columns), LANES)

    def landed(self, c, k, ref):
        pltpu.make_async_copy(ref.at[c], ref.at[c], self.rsem.at[c, k]).wait()


def kernel(*refs):
    (weight, first, second, mixing_in, target_in, mixed, factor, mixing, target, found,
     stage, done, pow_sent, pow_came, load_sem, out_sem, pow_ssem, pow_rsem), refs = refs[:18], refs[18:]
    _, rows, columns = stage.shape
    groups = []
    start = 0
    for spec in GROUPS:
        n = 5 + spec[0]
        groups.append(Group(spec, start, columns, refs[:n], refs[n:n + 2]))
        refs = refs[n + 2:]
        start += spec[2] * spec[3]
    section = lax.axis_index("section")
    tensor = lax.axis_index("tensor")
    z = section // 2
    half = lax.rem(section, 2)

    def plane(step):
        return lax.rem(z + (step + PLANES), PLANES)

    def along(step):
        return (plane(step) * 2 + half, tensor)

    def flip(bit):
        return (section, tensor + bit - 2 * bit * lax.rem(tensor // bit, 2))

    across = (z * 2 + 1 - half, tensor)
    partners = [flip(bit) for bit in (1, 8, 2, 4)]

    loads = [pltpu.make_async_copy(array.at[0], stage.at[a], load_sem.at[a])
             for a, array in enumerate((weight, first, second))]
    loads.append(pltpu.make_async_copy(mixing_in, mixing, load_sem.at[3]))
    loads.append(pltpu.make_async_copy(target_in, target, load_sem.at[4]))
    barrier = pltpu.get_barrier_semaphore()
    reach = max(max(group.before, group.after) for group in groups)
    peers = [along(way * step) for step in range(1, reach + 1) for way in (1, -1)] + [across] + partners
    for peer in peers:
        pl.semaphore_signal(barrier, inc=1, device_id=peer, device_id_type=MESH)
    for load in loads:
        load.start()

    def remote(g, src, dst, c, k, device):
        return pltpu.make_async_remote_copy(
            src_ref=src, dst_ref=dst, send_sem=g.ssem.at[k], recv_sem=g.rsem.at[c, k],
            device_id=device, device_id_type=MESH)

    def turn(g, c):
        a, col = g.where(c)
        for i in range(PLANES):
            slab = plane(i - (g.hubs + g.after - 1))
            g.own[c, i] = stage[a, :, pl.ds(pl.multiple_of(col + slab * g.width, LANES), g.width)]

    def do_first(g, c):
        for at, n, to, step in g.firsts:
            remote(g, g.own.at[c, pl.ds(at, n)], g.rl[0].at[c, pl.ds(to, n)], c, 0, along(step)).start()

    def do_start(g, c):
        turn(g, c)
        do_first(g, c)

    def do_pass(s, g, c):
        g.landed(c, s - 1, g.rl[s - 1])
        for at, to, n, step in g.passes[s - 1]:
            remote(g, g.rl[s - 1].at[c, pl.ds(at, n)], g.rl[s].at[c, pl.ds(to, n)], c, s, along(step)).start()

    def mix(g, c, place):
        squared = g.where(c)[0] == 2
        hub, step = g.targets[place]
        to = plane(step) * 2
        coefs = []
        for _, _, away in g.sources[hub]:
            layer = plane(away) * 2 + half
            for new in (2 * (to + half), 2 * (to + 1 - half)):
                for n in range(2):
                    coef = mixing[layer, new + n]
                    coefs.append(coef * jnp.where(squared, coef, 1.0))
        for lane in range(0, g.width, LANES):
            lanes = pl.ds(lane, LANES)
            sums = [None] * 4
            for i, (name, at, _) in enumerate(g.sources[hub]):
                old = (g.own if name == "own" else g.rl[name])[c, at, :, lanes]
                for n in range(4):
                    term = coefs[4 * i + n] * old
                    sums[n] = term if i == 0 else sums[n] + term
            for n in range(2):
                g.part[c, place, n, :, lanes] = sums[n]
                g.sent[c, place, n, :, lanes] = sums[2 + n]

    def do_mix(g, c):
        g.landed(c, g.hubs - 1, g.rl[g.hubs - 1])
        for at in (0, 4):
            for place in range(at, at + 4):
                mix(g, c, place)
            remote(g, g.sent.at[c, pl.ds(at, 4)], g.came.at[c, pl.ds(at, 4)], c, g.hubs, across).start()

    def do_join(g, c):
        g.landed(c, g.hubs, g.came)
        for i in range(g.arms):
            g.part[c, i] = g.part[c, i] + g.came[c, i]
            remote(g, g.part.at[c, i], g.back.at[c, i], c, g.hubs + 1, along(g.targets[i][1])).start()
        for i in range(g.arms, PLANES):
            g.part[c, i] = g.part[c, i] + g.came[c, i]

    def do_end(g, c):
        g.landed(c, g.hubs + 1, g.back)
        a, col = g.where(c)
        for role in range(PLANES):
            slab = plane(-role)
            lanes = pl.ds(pl.multiple_of(col + slab * g.width, LANES), g.width)
            name, at = g.finished[role]
            done[a, :, :, lanes] = (g.part if name == "part" else g.back)[c, at]
        lanes = pl.ds(col, g.chunk)
        pltpu.make_async_copy(done.at[a, :, :, lanes], mixed.at[a, :, :, lanes], out_sem.at[0]).start()

        @pl.when(a == 0)
        def _():
            for n in range(2):
                total = pow_sent[0, n]
                for lane in range(0, g.chunk, LANES):
                    for row in range(0, rows, 8):
                        value = done[0, n, pl.ds(row, 8), pl.ds(pl.multiple_of(col + lane, LANES), LANES)]
                        total = total + value * value
                pow_sent[0, n] = total

    def pow_copy(k):
        return pltpu.make_async_remote_copy(
            src_ref=pow_sent.at[k], dst_ref=pow_came.at[k], send_sem=pow_ssem.at[k], recv_sem=pow_rsem.at[k],
            device_id=partners[k], device_id_type=MESH)

    factor_copy = pltpu.make_async_copy(found, factor, load_sem.at[5])

    def do_factor():
        total_count = rows * lax.axis_size("tensor") * columns
        for n in range(2):
            total = jnp.sum(pow_sent[len(partners), n], keepdims=True)
            value = 1.0 / jnp.sqrt(total / total_count + 1e-06)
            scale = target[n] * value[0, 0]
            found[0, n] = scale
            found[1, n] = scale * scale
        factor_copy.start()

    pow_sent[0] = jnp.zeros_like(pow_sent[0])
    loads[0].wait()
    for c in range(LEAD):
        turn(groups[0], c)
    pl.semaphore_wait(barrier, len(peers))
    for c in range(LEAD):
        do_first(groups[0], c)
    for load in loads[1:]:
        load.wait()

    steps = []
    for kind in ORDER:
        for i, g in enumerate(groups):
            if kind == "first":
                steps.append((g, g.base - (0 if i else LEAD) * g.stride, 0 if i else LEAD, do_start))
            elif kind == "pass":
                for s in range(1, g.hubs):
                    steps.append((g, g.base + g.lags[s - 1], 0, lambda g, c, s=s: do_pass(s, g, c)))
            else:
                at, step = {"mix": (-3, do_mix), "join": (-2, do_join), "end": (-1, do_end)}[kind]
                steps.append((g, g.base + g.lags[at], 0, step))
    pow_turn = max(g.base + g.lags[-1] + (min(g.count, (columns - g.start) // g.chunk) - 1) * g.stride
                   for g in groups if g.start < columns)
    turns = max([g.base + g.lags[-1] + (g.count - 1) * g.stride + 1 for g in groups] + [pow_turn + POW_LAG * len(partners) + 1])

    def turn_of(t, _):
        for g, lag, least, step in steps:
            c = (t - lag) // g.stride if g.stride > 1 else t - lag
            on_turn = (t - lag >= 0) & (c >= least) & (c < g.count)
            if g.stride > 1:
                on_turn &= lax.rem(t - lag, g.stride) == 0

            @pl.when(on_turn)
            def _(g=g, c=c, step=step):
                step(g, c)

        for k in range(len(partners) + 1):
            @pl.when(t == pow_turn + POW_LAG * k)
            def _(k=k):
                if k > 0:
                    pow_copy(k - 1).wait()
                    pow_sent[k] = pow_sent[k - 1] + pow_came[k - 1]
                if k < len(partners):
                    pow_copy(k).start()
                else:
                    do_factor()
        return 0

    lax.fori_loop(0, turns, turn_of, 0)

    for g in groups:
        for k, ref in enumerate((*g.rl, g.came, g.back)):
            pltpu.make_async_copy(ref, ref, g.ssem.at[k]).wait()
    pltpu.make_async_copy(done, done, out_sem.at[0]).wait()
    factor_copy.wait()


def scaled(factor_in, mixed, new_weight, new_first, new_second, factor, held, factor_sem, in_sem, out_sem):
    factor_copy = pltpu.make_async_copy(factor_in, factor, factor_sem.at[0])
    factor_copy.start()
    parts = [(a, n) for a in range(3) for n in range(2)]
    for a, n in parts:
        pltpu.make_async_copy(mixed.at[a, n], held.at[a, n], in_sem.at[a, n]).start()
    factor_copy.wait()
    outs = (new_weight, new_first, new_second)
    for a, n in parts:
        pltpu.make_async_copy(mixed.at[a, n], held.at[a, n], in_sem.at[a, n]).wait()
        scale = factor[1 if a == 2 else 0, n]
        held[a, n] = held[a, n] * scale
        pltpu.make_async_copy(held.at[a, n], outs[a].at[n], out_sem.at[a, n]).start()
    for a, n in parts:
        pltpu.make_async_copy(held.at[a, n], outs[a].at[n], out_sem.at[a, n]).wait()


def local(old_weight, old_first, old_second, mixing, target_rms):
    rows, columns = old_weight.shape[1:]
    hbm = pl.BlockSpec(memory_space=pltpu.HBM)
    dma = pltpu.SemaphoreType.DMA
    scratch = []
    for hubs, before, chunk, n, _, _, _ in GROUPS:
        sizes = plan(hubs, before)[0]
        w = chunk // PLANES
        for k in (PLANES,):
            scratch.append(pltpu.VMEM((n, k, rows, w), F32))
        for k in (PLANES, PLANES, PLANES, PLANES - hubs):
            scratch.append(pltpu.VMEM((n, k, 2, rows, w), F32))
        for size in sizes:
            scratch.append(pltpu.VMEM((n, size, rows, w), F32))
        scratch += [dma((hubs + 2,)), dma((n, hubs + 2))]
    mixed, factor = pl.pallas_call(
        kernel,
        out_shape=(
            jax.ShapeDtypeStruct((3, 2, rows, columns), F32),
            jax.ShapeDtypeStruct((2, 2), F32),
        ),
        in_specs=[hbm] * 5,
        out_specs=(hbm, hbm),
        scratch_shapes=[
            pltpu.SMEM(mixing.shape[::-1], F32), pltpu.SMEM(target_rms.shape, F32), pltpu.SMEM((2, 2), F32),
            pltpu.VMEM((3, rows, columns), F32), pltpu.VMEM((3, 2, rows, columns), F32),
            pltpu.VMEM((5, 2, 8, LANES), F32), pltpu.VMEM((4, 2, 8, LANES), F32),
            dma((6,)), dma((1,)), dma((4,)), dma((4,)), *scratch,
        ],
        compiler_params=pltpu.CompilerParams(
            collective_id=0, has_side_effects=True, vmem_limit_bytes=60 << 20),
        name="grow",
    )(old_weight, old_first, old_second, mixing.T, target_rms)
    new = jax.ShapeDtypeStruct((2, rows, columns), F32)
    return pl.pallas_call(
        scaled,
        out_shape=(new, new, new),
        in_specs=[hbm, hbm],
        out_specs=(hbm, hbm, hbm),
        scratch_shapes=[
            pltpu.SMEM((2, 2), F32), pltpu.VMEM((3, 2, rows, columns), F32),
            dma((1,)), dma((3, 2)), dma((3, 2)),
        ],
        compiler_params=pltpu.CompilerParams(vmem_limit_bytes=60 << 20),
        name="scale",
    )(factor, mixed)


def solution(mesh):
    split = P("section", "tensor", None)
    return jax.shard_map(
        local,
        mesh=mesh,
        in_specs=(split, split, split, P(), P("section")),
        out_specs=(split, split, split),
        check_vma=False,
    )
```
